32 devices in a mesh: blk: 16 (over z, x, core), slab: 2 (over y).
Axes of the slice: x: 2, y: 2, z: 4, core: 2. Of those that a mesh axis runs over, the one named last changes fastest.
Arguments:
- tokens: bfloat16 [524288, 128], P(('blk', 'slab')), may hold values from -6 to 6
- listed: int32 [2048, 3], P(('blk', 'slab')), may hold values from 0 to 511, as said below
- centroids: bfloat16 [131072, 128], P('blk'), may hold values from -6 to 6
Outputs:
- refined: float32 [131072, 128], P(('blk', 'slab'))
- counts: float32 [131072], P(('blk', 'slab'))
The draws below stay inside these ranges and needn't reach their ends.
Inputs may be any that keep to these rules, and one draw needn't show every extreme that they name: `listed`: in the rows of one device (64 token blocks), all ids of one owner group (id // 32) are equal, so a device names at most one block of each owner group. The three ids of a row are distinct.
All inputs are finite; a program needn't handle non-finite values.
Results may differ from the reference program's by a relative error of at most 0.00093.
Values may be sent and summed in bfloat16 or wider, within the bound.
A program may use at most 128 MiB of HBM per device.

```python
import jax
import jax.numpy as jnp
from jax import lax

EMBED_WIDTH = 128
CENT_BLK = 256
TOK_BLK = 256
BPO = 32
TBD = 64
USED = 12
CENTROIDS = 131072
TOKENS = 524288
N_BLK = 16
N_SLAB = 2


def draw_listed(key, part):
    device_count = N_BLK * N_SLAB
    hot_key = jax.random.fold_in(key, 11)
    label_key = jax.random.fold_in(key, 12)
    within_key = jax.random.fold_in(key, 13)
    pick_key = jax.random.fold_in(key, 14)
    hot_owner = jax.random.randint(hot_key, (N_SLAB,), 0, N_BLK)
    device_keys = jax.random.split(label_key, device_count)
    other_labels = jax.vmap(lambda row_key: jax.random.permutation(row_key, N_BLK - 1)[:USED - 1] + 1)(device_keys)
    owner_labels = jnp.concatenate([jnp.zeros((device_count, 1), jnp.int32), other_labels.astype(jnp.int32)], axis=1)
    slab_of = jnp.arange(device_count, dtype=jnp.int32) % N_SLAB
    owner_lookup = (owner_labels + hot_owner[slab_of][:, None]) % N_BLK
    within_ids = jax.random.randint(within_key, (device_count, USED), 0, BPO)
    block_table = owner_lookup * BPO + within_ids
    row_keys = jax.random.split(pick_key, device_count * TBD)
    picked_slots = jax.vmap(lambda row_key: jax.random.permutation(row_key, USED)[:3])(row_keys)
    device_of = jnp.arange(device_count * TBD, dtype=jnp.int32) // TBD
    chosen = block_table[device_of[:, None], picked_slots]
    return chosen.astype(jnp.int32)


def block_levels(rng, extent, shards, smallest, high):
    def one(axis_at, blocks):
        heights = jax.random.uniform(jax.random.fold_in(jax.random.fold_in(rng, 6), axis_at), (blocks,), jnp.float32, smallest / len(shards), high / len(shards))
        return jnp.repeat(jnp.exp(heights), extent[axis_at] // blocks).reshape((-1,) + (1,) * (len(extent) - axis_at - 1))

    gain = one(*shards[0])
    for cut in shards[1:]:
        gain = gain * one(*cut)
    return gain


def gaussian(stream_key, extent, scale, most, pieces=(), held_as=jnp.bfloat16):
    drawn = scale * jax.random.normal(stream_key, extent, jnp.float32)
    if pieces:
        drawn = drawn * block_levels(stream_key, extent, pieces, -0.22, 0.18)
    return jnp.clip(drawn, -most, most).astype(held_as)


def setup_inputs(seed: int = 0) -> dict:
    keys = jax.random.split(jax.random.key(seed), 4)
    return {
        "tokens": gaussian(keys[0], (TOKENS, EMBED_WIDTH), 1.0, 6.0, ((0, 32),)),
        "listed": draw_listed(jax.random.fold_in(keys[3], 71), 0),
        "centroids": gaussian(keys[2], (CENTROIDS, EMBED_WIDTH), 1.0, 6.0, ((0, 16),)),
    }


SOFTMAX_TEMP = 0.1
PRIOR_WEIGHT = 4.0
EPSILON = 1e-06

def unit_rows(values):
    widened = values.astype(jnp.float32)
    return widened * lax.rsqrt(lax.optimization_barrier(jnp.mean(widened * widened, axis=-1, keepdims=True)) + EPSILON)

def reference(tokens, listed, centroids):
    centroid_norm = unit_rows(centroids)
    cent_round = lax.optimization_barrier(centroid_norm.astype(jnp.bfloat16))
    cent_round = cent_round.astype(jnp.float32).reshape(-1, CENT_BLK, EMBED_WIDTH)
    tok_round = lax.optimization_barrier(unit_rows(tokens).astype(jnp.bfloat16))
    tok_round = tok_round.astype(jnp.float32).reshape(-1, TOK_BLK, EMBED_WIDTH)
    nblocks = listed.shape[0]
    batch = 32
    total_blocks = cent_round.shape[0]

    def accumulate(state_pair, turn_index):
        sum_acc, count_acc = state_pair
        start = (turn_index * batch).astype(jnp.int32)
        token_rows = lax.dynamic_slice_in_dim(tok_round, start, batch, 0)
        block_ids = lax.dynamic_slice_in_dim(listed, start, batch, 0)
        candidate_centroids = cent_round[block_ids].reshape(batch, 3 * CENT_BLK, EMBED_WIDTH)
        score_matrix = jnp.einsum('wsy,way->wsa', token_rows, candidate_centroids) / (EMBED_WIDTH * SOFTMAX_TEMP)
        weights = jnp.exp(score_matrix)
        weights = weights / lax.optimization_barrier(jnp.sum(weights, axis=-1, keepdims=True))
        weights_low = lax.optimization_barrier(weights.astype(jnp.bfloat16)).astype(jnp.float32)
        weights_low = weights_low.reshape(batch, TOK_BLK, 3, CENT_BLK)
        partial_value = jnp.einsum('gtkc,gtd->gkcd', weights_low, token_rows)
        part_counts = lax.optimization_barrier(jnp.sum(weights.reshape(batch, TOK_BLK, 3, CENT_BLK), axis=1))
        flat_ids = block_ids.reshape(-1)
        sum_acc = sum_acc.at[flat_ids].add(partial_value.reshape(-1, CENT_BLK, EMBED_WIDTH))
        count_acc = count_acc.at[flat_ids].add(part_counts.reshape(-1, CENT_BLK))
        return ((sum_acc, count_acc), None)
    start_pair = (jnp.zeros((total_blocks, CENT_BLK, EMBED_WIDTH), jnp.float32), jnp.zeros((total_blocks, CENT_BLK), jnp.float32))
    (sum_acc, count_acc), _ = lax.scan(accumulate, start_pair, jnp.arange(nblocks // batch, dtype=jnp.int32))
    sum_flat = sum_acc.reshape(-1, EMBED_WIDTH)
    count_flat = count_acc.reshape(-1)
    refined = (sum_flat + PRIOR_WEIGHT * centroid_norm) / (count_flat[:, None] + PRIOR_WEIGHT)
    return (refined, count_flat)
```

```python
import functools
import math

import jax
import jax.numpy as jnp
from jax import lax
from jax.experimental import pallas as pl
from jax.experimental.pallas import tpu as pltpu
from jax.sharding import PartitionSpec as P

CENT_BLK = 256
TOK_BLK = 256
SOFTMAX_TEMP = 0.1
PRIOR_WEIGHT = 4.0
EPSILON = 1e-06
LEVELS = 32767.0
MESH = pl.DeviceIdType.MESH


def unit_rows(values):
    widened = values.astype(jnp.float32)
    return widened * lax.rsqrt(jnp.mean(widened * widened, axis=-1, keepdims=True) + EPSILON)


def greet(peers):
    barrier = pltpu.get_barrier_semaphore()
    for peer in peers:
        pl.semaphore_signal(barrier, inc=1, device_id=peer, device_id_type=MESH)
    pl.semaphore_wait(barrier, len(peers))


def fetch_kernel(owners, listed_ref, cent_ref, out_ref, req_ref, asked_v, asked_s, reply,
                 ask_send, ask_recv, ask_local, rep_send, rep_recv, own_sem):
    me = lax.axis_index("blk")
    slab = lax.axis_index("slab")
    per_owner = cent_ref.shape[0]

    lanes = lax.broadcasted_iota(jnp.int32, (listed_ref.shape[0], 128), 1)
    best = jnp.zeros((1, 128), jnp.int32)
    for j in range(listed_ref.shape[1]):
        inner = listed_ref[:, j : j + 1] - lanes * per_owner
        held = jnp.where((inner >= 0) & (inner < per_owner), inner + 1, 0)
        best = jnp.maximum(best, jnp.max(held, axis=0, keepdims=True))
    req_ref[...] = jnp.broadcast_to(best, req_ref.shape)

    greet([(lax.rem(me + off, owners), slab) for off in range(1, owners)])

    def ask(off):
        return pltpu.make_async_remote_copy(
            src_ref=req_ref, dst_ref=asked_v.at[me], send_sem=ask_send.at[off], recv_sem=ask_recv.at[off],
            device_id=(lax.rem(me + off, owners), slab), device_id_type=MESH)

    def asked_by(off):
        src = lax.rem(me - off + owners, owners)
        return pltpu.make_async_remote_copy(
            src_ref=req_ref, dst_ref=asked_v.at[src], send_sem=ask_send.at[off], recv_sem=ask_recv.at[off],
            device_id=(src, slab), device_id_type=MESH)

    def give(off):
        return pltpu.make_async_remote_copy(
            src_ref=reply.at[off], dst_ref=out_ref.at[me], send_sem=rep_send.at[off], recv_sem=rep_recv.at[off],
            device_id=(lax.rem(me - off + owners, owners), slab), device_id_type=MESH)

    def given_by(off):
        src = lax.rem(me + off, owners)
        return pltpu.make_async_remote_copy(
            src_ref=reply.at[off], dst_ref=out_ref.at[src], send_sem=rep_send.at[off], recv_sem=rep_recv.at[off],
            device_id=(src, slab), device_id_type=MESH)

    def answer(off, source, src):
        pull = pltpu.make_async_copy(source, asked_s.at[src], ask_local)
        pull.start()
        pull.wait()
        wanted = jnp.maximum(asked_s[src, 0, me] - 1, 0)
        reply[off] = unit_rows(cent_ref[wanted]).astype(jnp.bfloat16)

    @pl.loop(1, owners)
    def _(off):
        ask(off).start()

    answer(0, req_ref, me)
    own = pltpu.make_async_copy(reply.at[0], out_ref.at[me], own_sem)
    own.start()

    @pl.loop(1, owners)
    def _(off):
        src = lax.rem(me - off + owners, owners)
        asked_by(off).wait_recv()
        answer(off, asked_v.at[src], src)
        give(off).start()

    own.wait()

    @pl.loop(1, owners)
    def _(off):
        ask(off).wait_send()
        give(off).wait_send()
        given_by(off).wait_recv()


def softmax_kernel(group, slots_ref, req_ref, tok_ref, cent_ref, q_ref, meta_ref, total, mass):
    step = pl.program_id(0)
    owners = cent_ref.shape[0]
    width = tok_ref.shape[-1]
    factor = math.log2(math.e) / (width * SOFTMAX_TEMP)

    @pl.when(step == 0)
    def _():
        total[...] = jnp.zeros_like(total)
        mass[...] = jnp.zeros_like(mass)

    for g in range(group):
        tok = unit_rows(tok_ref[g]).astype(jnp.bfloat16)
        slots = [slots_ref[(step * group + g) * 3 + j] for j in range(3)]
        grown = []
        norm = jnp.zeros((1, TOK_BLK), jnp.float32)
        for slot in slots:
            scores = lax.dot_general(cent_ref[slot], tok, (((1,), (1,)), ((), ())),
                                     preferred_element_type=jnp.float32)
            grown.append(jnp.exp2(scores * factor))
            norm = norm + jnp.sum(grown[-1], axis=0, keepdims=True)
        scale = 1.0 / norm
        for slot, value in zip(slots, grown):
            weights = value * scale
            part = weights[:, :128]
            for lane in range(128, TOK_BLK, 128):
                part = part + weights[:, lane : lane + 128]
            mass[slot] += part
            total[slot] += jnp.dot(weights.astype(jnp.bfloat16), tok, preferred_element_type=jnp.float32)

    @pl.when(step == pl.num_programs(0) - 1)
    def _():
        lanes = lax.broadcasted_iota(jnp.int32, (CENT_BLK, 128), 1)
        table = jnp.zeros((CENT_BLK, 128), jnp.float32)
        for k in range(owners):
            sums = total[k]
            top = jnp.max(jnp.abs(sums), axis=1, keepdims=True)
            inverse = LEVELS / jnp.maximum(top, 1e-30)
            q_ref[k] = jnp.floor(sums * inverse + 0.5).astype(jnp.int32).astype(jnp.int16)
            count = jnp.sum(mass[k], axis=1, keepdims=True)
            wanted = jnp.maximum(req_ref[k] - 1, 0).astype(jnp.float32)
            table = jnp.where(lanes == k, top * (1.0 / LEVELS), table)
            table = jnp.where(lanes == owners + k, count, table)
            table = jnp.where(lanes == 2 * owners + k, wanted, table)
        turned = table.T
        for kind in range(3):
            meta_ref[:, kind, :] = turned[kind * owners : (kind + 1) * owners]
        for kind in range(3, 8):
            meta_ref[:, kind, :] = jnp.zeros((owners, CENT_BLK), jnp.float32)


def return_kernel(owners, slabs, q_ref, meta_ref, q_out, meta_out, send_sem, recv_sem, fwd_send, fwd_recv, own_sem):
    me = lax.axis_index("blk")
    slab = lax.axis_index("slab")
    greet([(lax.rem(me + off, owners), slab) for off in range(1, owners)]
          + [(me, lax.rem(slab + t, slabs)) for t in range(1, slabs)])
    pairs = ((q_ref, q_out), (meta_ref, meta_out))

    def give(kind, off):
        dest = lax.rem(me + off, owners)
        source, target = pairs[kind]
        return pltpu.make_async_remote_copy(
            src_ref=source.at[dest], dst_ref=target.at[slab, me], send_sem=send_sem.at[kind, off],
            recv_sem=recv_sem.at[kind, off], device_id=(dest, slab), device_id_type=MESH)

    def given(kind, off):
        src = lax.rem(me - off + owners, owners)
        source, target = pairs[kind]
        return pltpu.make_async_remote_copy(
            src_ref=source.at[src], dst_ref=target.at[slab, src], send_sem=send_sem.at[kind, off],
            recv_sem=recv_sem.at[kind, off], device_id=(src, slab), device_id_type=MESH)

    def forward(kind, off, t):
        src = lax.rem(me - off + owners, owners)
        target = pairs[kind][1]
        return pltpu.make_async_remote_copy(
            src_ref=target.at[slab, src], dst_ref=target.at[slab, src], send_sem=fwd_send.at[kind, t, off],
            recv_sem=fwd_recv.at[kind, t, off], device_id=(me, lax.rem(slab + t, slabs)), device_id_type=MESH)

    def forwarded(kind, off, t):
        src = lax.rem(me - off + owners, owners)
        peer = lax.rem(slab - t + slabs, slabs)
        target = pairs[kind][1]
        return pltpu.make_async_remote_copy(
            src_ref=target.at[peer, src], dst_ref=target.at[peer, src], send_sem=fwd_send.at[kind, t, off],
            recv_sem=fwd_recv.at[kind, t, off], device_id=(me, peer), device_id_type=MESH)

    @pl.loop(1, owners)
    def _(off):
        for kind in range(2):
            give(kind, off).start()

    for kind in range(2):
        source, target = pairs[kind]
        own = pltpu.make_async_copy(source.at[me], target.at[slab, me], own_sem.at[kind])
        own.start()
        own.wait()
        for t in range(1, slabs):
            forward(kind, 0, t).start()

    @pl.loop(1, owners)
    def _(off):
        for kind in range(2):
            given(kind, off).wait_recv()
            for t in range(1, slabs):
                forward(kind, off, t).start()

    @pl.loop(1, owners)
    def _(off):
        for kind in range(2):
            give(kind, off).wait_send()

    @pl.loop(0, owners)
    def _(off):
        for kind in range(2):
            for t in range(1, slabs):
                forward(kind, off, t).wait_send()
                forwarded(kind, off, t).wait_recv()


def finish_kernel(ids_ref, q_ref, meta_ref, cent_ref, out_ref, count_ref):
    contributions = q_ref.shape[0]
    share = cent_ref.shape[0]
    first = ids_ref[contributions] * share
    out_ref[...] = PRIOR_WEIGHT * unit_rows(cent_ref[...])
    count_ref[...] = jnp.zeros_like(count_ref)
    for start in range(0, contributions, 128):
        many = min(128, contributions - start)
        rows = meta_ref[start : start + many, 0, :]
        if many < 128:
            rows = jnp.concatenate([rows, jnp.zeros((128 - many, CENT_BLK), jnp.float32)], axis=0)
        scales = rows.T
        for k in range(many):
            inner = ids_ref[start + k] - first

            @pl.when((inner >= 0) & (inner < share))
            def _():
                out_ref[inner] += q_ref[start + k].astype(jnp.float32) * scales[:, k : k + 1]
                count_ref[pl.ds(inner, 1), :] += meta_ref[start + k, 1:2, :]

    masses = jnp.concatenate([count_ref[...], jnp.zeros((128 - share, CENT_BLK), jnp.float32)], axis=0).T
    for i in range(share):
        out_ref[i] = out_ref[i] / (masses[:, i : i + 1] + PRIOR_WEIGHT)


def shards(owners, slabs, tokens, listed, centroids):
    width = tokens.shape[-1]
    blocks = listed.shape[0]
    per_owner = centroids.shape[0] // CENT_BLK
    share = per_owner // slabs
    cents = centroids.reshape(per_owner, CENT_BLK, width)
    vmem = pl.BlockSpec(memory_space=pltpu.VMEM)
    anywhere = pl.BlockSpec(memory_space=pl.ANY)
    dma = pltpu.SemaphoreType.DMA

    fetched, req = pl.pallas_call(
        functools.partial(fetch_kernel, owners),
        out_shape=(jax.ShapeDtypeStruct((owners, CENT_BLK, width), jnp.bfloat16),
                   jax.ShapeDtypeStruct((8, 128), jnp.int32)),
        in_specs=[vmem, vmem],
        out_specs=(anywhere, vmem),
        scratch_shapes=[
            pltpu.VMEM((owners, 8, 128), jnp.int32),
            pltpu.SMEM((owners, 8, 128), jnp.int32),
            pltpu.VMEM((owners, CENT_BLK, width), jnp.bfloat16),
            dma((owners,)), dma((owners,)), dma, dma((owners,)), dma((owners,)), dma,
        ],
        compiler_params=pltpu.CompilerParams(
            collective_id=0, has_side_effects=True, vmem_limit_bytes=16 * 2**20),
        name="fetch",
    )(listed, cents)

    group = 2
    packed, meta = pl.pallas_call(
        functools.partial(softmax_kernel, group),
        out_shape=(jax.ShapeDtypeStruct((owners, CENT_BLK, width), jnp.int16),
                   jax.ShapeDtypeStruct((owners, 8, CENT_BLK), jnp.float32)),
        grid_spec=pltpu.PrefetchScalarGridSpec(
            num_scalar_prefetch=2,
            grid=(blocks // group,),
            in_specs=[
                pl.BlockSpec((group, TOK_BLK, width), lambda i, *_: (i, 0, 0)),
                pl.BlockSpec((owners, CENT_BLK, width), lambda i, *_: (0, 0, 0)),
            ],
            out_specs=[
                pl.BlockSpec((owners, CENT_BLK, width), lambda i, *_: (0, 0, 0)),
                pl.BlockSpec((owners, 8, CENT_BLK), lambda i, *_: (0, 0, 0)),
            ],
            scratch_shapes=[
                pltpu.VMEM((owners, CENT_BLK, width), jnp.float32),
                pltpu.VMEM((owners, CENT_BLK, 128), jnp.float32),
            ],
        ),
        compiler_params=pltpu.CompilerParams(
            dimension_semantics=("arbitrary",), vmem_limit_bytes=40 * 2**20),
        name="softmax",
    )((listed // per_owner).reshape(-1), req[0], tokens.reshape(blocks, TOK_BLK, width), fetched)

    q_all, meta_all = pl.pallas_call(
        functools.partial(return_kernel, owners, slabs),
        out_shape=(jax.ShapeDtypeStruct((slabs, owners, CENT_BLK, width), jnp.int16),
                   jax.ShapeDtypeStruct((slabs, owners, 8, CENT_BLK), jnp.float32)),
        in_specs=[anywhere, anywhere],
        out_specs=(anywhere, anywhere),
        scratch_shapes=[dma((2, owners)), dma((2, owners)), dma((2, slabs, owners)), dma((2, slabs, owners)), dma((2,))],
        compiler_params=pltpu.CompilerParams(collective_id=1, has_side_effects=True),
        name="give_back",
    )(packed, meta)

    contributions = slabs * owners
    meta_flat = meta_all.reshape(contributions, 8, CENT_BLK)
    ids = jnp.concatenate([meta_flat[:, 2, 0].astype(jnp.int32), lax.axis_index("slab").astype(jnp.int32)[None]])
    refined, counts = pl.pallas_call(
        finish_kernel,
        out_shape=(jax.ShapeDtypeStruct((share, CENT_BLK, width), jnp.float32),
                   jax.ShapeDtypeStruct((share, CENT_BLK), jnp.float32)),
        grid_spec=pltpu.PrefetchScalarGridSpec(
            num_scalar_prefetch=1,
            grid=(1,),
            in_specs=[
                pl.BlockSpec((contributions, CENT_BLK, width), lambda i, *_: (0, 0, 0)),
                pl.BlockSpec((contributions, 8, CENT_BLK), lambda i, *_: (0, 0, 0)),
                pl.BlockSpec((share, CENT_BLK, width), lambda i, ids: (ids[contributions], 0, 0)),
            ],
            out_specs=[
                pl.BlockSpec((share, CENT_BLK, width), lambda i, *_: (0, 0, 0)),
                pl.BlockSpec((share, CENT_BLK), lambda i, *_: (0, 0)),
            ],
        ),
        compiler_params=pltpu.CompilerParams(
            dimension_semantics=("arbitrary",), vmem_limit_bytes=56 * 2**20),
        name="finish",
    )(ids, q_all.reshape(contributions, CENT_BLK, width), meta_flat, cents)
    return refined.reshape(share * CENT_BLK, width), counts.reshape(share * CENT_BLK)


def solution(mesh):
    placed = (P(("blk", "slab"), None), P(("blk", "slab"), None), P("blk", None))
    return jax.shard_map(
        functools.partial(shards, mesh.shape["blk"], mesh.shape["slab"]),
        mesh=mesh,
        in_specs=placed,
        out_specs=(P(("blk", "slab"), None), P(("blk", "slab"))),
        check_vma=False,
    )
```

```python
import functools
import math

import jax
import jax.numpy as jnp
from jax import lax
from jax.experimental import pallas as pl
from jax.experimental.pallas import tpu as pltpu
from jax.sharding import PartitionSpec as P

CENT_BLK = 256
TOK_BLK = 256
SOFTMAX_TEMP = 0.1
PRIOR_WEIGHT = 4.0
EPSILON = 1e-06
LEVELS = 32767.0
MESH = pl.DeviceIdType.MESH


def unit_rows(values):
    widened = values.astype(jnp.float32)
    return widened * lax.rsqrt(jnp.mean(widened * widened, axis=-1, keepdims=True) + EPSILON)


def partner(me, off, count):
    assert count & (count - 1) == 0
    other = 0
    bit = 1
    while bit < count:
        mine = lax.rem(me // bit, 2)
        other = other + bit * (1 - mine if off & bit else mine)
        bit *= 2
    return other


def greet(peers):
    barrier = pltpu.get_barrier_semaphore()
    for peer in peers:
        pl.semaphore_signal(barrier, inc=1, device_id=peer, device_id_type=MESH)
    pl.semaphore_wait(barrier, len(peers))


def fetch_kernel(owners, listed_ref, cent_ref, out_ref, req_ref, asked_v, asked_s, reply,
                 ask_send, ask_recv, ask_local, rep_send, rep_recv, own_sem):
    me = lax.axis_index("blk")
    slab = lax.axis_index("slab")
    per_owner = cent_ref.shape[0]

    lanes = lax.broadcasted_iota(jnp.int32, (listed_ref.shape[0], 128), 1)
    best = jnp.zeros((1, 128), jnp.int32)
    for j in range(listed_ref.shape[1]):
        inner = listed_ref[:, j : j + 1] - lanes * per_owner
        held = jnp.where((inner >= 0) & (inner < per_owner), inner + 1, 0)
        best = jnp.maximum(best, jnp.max(held, axis=0, keepdims=True))
    req_ref[...] = jnp.broadcast_to(best, req_ref.shape)

    greet([(partner(me, off, owners), slab) for off in range(1, owners)])

    def ask(off):
        return pltpu.make_async_remote_copy(
            src_ref=req_ref, dst_ref=asked_v.at[me], send_sem=ask_send.at[off], recv_sem=ask_recv.at[off],
            device_id=(partner(me, off, owners), slab), device_id_type=MESH)

    def asked_by(off):
        src = partner(me, off, owners)
        return pltpu.make_async_remote_copy(
            src_ref=req_ref, dst_ref=asked_v.at[src], send_sem=ask_send.at[off], recv_sem=ask_recv.at[off],
            device_id=(src, slab), device_id_type=MESH)

    def give(off):
        return pltpu.make_async_remote_copy(
            src_ref=reply.at[off], dst_ref=out_ref.at[me], send_sem=rep_send.at[off], recv_sem=rep_recv.at[off],
            device_id=(partner(me, off, owners), slab), device_id_type=MESH)

    def given_by(off):
        src = partner(me, off, owners)
        return pltpu.make_async_remote_copy(
            src_ref=reply.at[off], dst_ref=out_ref.at[src], send_sem=rep_send.at[off], recv_sem=rep_recv.at[off],
            device_id=(src, slab), device_id_type=MESH)

    far_first = list(range(owners - 1, 0, -1))
    for off in far_first:
        ask(off).start()
    asked_v[me] = req_ref[...]
    for off in far_first:
        asked_by(off).wait_recv()
    pull = pltpu.make_async_copy(asked_v.at[:, 0], asked_s, ask_local)
    pull.start()
    pull.wait()
    own = pltpu.make_async_copy(reply.at[0], out_ref.at[me], own_sem)
    for off in far_first + [0]:
        wanted = jnp.maximum(asked_s[partner(me, off, owners), me] - 1, 0)
        reply[off] = unit_rows(cent_ref[wanted]).astype(jnp.bfloat16)
        (give(off) if off else own).start()
    own.wait()
    for off in far_first:
        ask(off).wait_send()
        give(off).wait_send()
        given_by(off).wait_recv()


def softmax_kernel(group, slots_ref, req_ref, tok_ref, cent_ref, q_ref, meta_ref, total, mass, grown, tok_held, scales):
    step = pl.program_id(0)
    owners = cent_ref.shape[0]
    width = tok_ref.shape[-1]
    factor = math.log2(math.e) / (width * SOFTMAX_TEMP)

    @pl.when(step == 0)
    def _():
        total[...] = jnp.zeros_like(total)
        mass[...] = jnp.zeros_like(mass)
        grown[1] = jnp.zeros_like(grown[1])
        tok_held[1] = jnp.zeros_like(tok_held[1])
        scales[1] = jnp.zeros_like(scales[1])

    def collect(block, side):
        tok = tok_held[side]
        scale = scales[side, 0:1]
        for j in range(3):
            slot = slots_ref[block * 3 + j]
            weights = grown[side, j] * scale
            part = weights[:, :128]
            for lane in range(128, TOK_BLK, 128):
                part = part + weights[:, lane : lane + 128]
            mass[slot] += part
            total[slot] += jnp.dot(weights.astype(jnp.bfloat16), tok, preferred_element_type=jnp.float32)

    def grow(block, g, side):
        tok = unit_rows(tok_ref[g]).astype(jnp.bfloat16)
        tok_held[side] = tok
        norm = jnp.zeros((1, TOK_BLK), jnp.float32)
        for j in range(3):
            scores = lax.dot_general(cent_ref[slots_ref[block * 3 + j]], tok, (((1,), (1,)), ((), ())),
                                     preferred_element_type=jnp.float32)
            value = jnp.exp2(scores * factor)
            grown[side, j] = value
            norm = norm + jnp.sum(value, axis=0, keepdims=True)
        scales[side] = jnp.broadcast_to(1.0 / norm, (8, TOK_BLK))

    for g in range(group):
        block = step * group + g
        collect(jnp.maximum(block - 1, 0), (g + 1) % 2)
        grow(block, g, g % 2)

    @pl.when(step == pl.num_programs(0) - 1)
    def _():
        collect(step * group + group - 1, (group + 1) % 2)
        lanes = lax.broadcasted_iota(jnp.int32, (CENT_BLK, 128), 1)
        table = jnp.zeros((CENT_BLK, 128), jnp.float32)
        for k in range(owners):
            sums = total[k]
            top = jnp.max(jnp.abs(sums), axis=1, keepdims=True)
            inverse = LEVELS / jnp.maximum(top, 1e-30)
            q_ref[k] = jnp.floor(sums * inverse + 0.5).astype(jnp.int32).astype(jnp.int16)
            count = jnp.sum(mass[k], axis=1, keepdims=True)
            wanted = jnp.maximum(req_ref[k] - 1, 0).astype(jnp.float32)
            table = jnp.where(lanes == k, top * (1.0 / LEVELS), table)
            table = jnp.where(lanes == owners + k, count, table)
            table = jnp.where(lanes == 2 * owners + k, wanted, table)
        turned = table.T
        for kind in range(3):
            rows = turned[kind * owners : (kind + 1) * owners]
            for half in range(CENT_BLK // 128):
                meta_ref[:, 2 * kind + half, :] = rows[:, half * 128 : (half + 1) * 128]
        meta_ref[:, 6:, :] = jnp.zeros((owners, 2, 128), jnp.float32)


def return_kernel(owners, slabs, q_ref, meta_ref, q_out, meta_out, send_sem, recv_sem, fwd_send, fwd_recv, own_sem):
    me = lax.axis_index("blk")
    slab = lax.axis_index("slab")
    greet([(partner(me, off, owners), slab) for off in range(1, owners)]
          + [(me, lax.rem(slab + t, slabs)) for t in range(1, slabs)])
    pairs = ((q_ref, q_out), (meta_ref, meta_out))

    def give(kind, off):
        dest = partner(me, off, owners)
        source, target = pairs[kind]
        return pltpu.make_async_remote_copy(
            src_ref=source.at[dest], dst_ref=target.at[slab, me], send_sem=send_sem.at[kind, off],
            recv_sem=recv_sem.at[kind, off], device_id=(dest, slab), device_id_type=MESH)

    def given(kind, off):
        src = partner(me, off, owners)
        source, target = pairs[kind]
        return pltpu.make_async_remote_copy(
            src_ref=source.at[src], dst_ref=target.at[slab, src], send_sem=send_sem.at[kind, off],
            recv_sem=recv_sem.at[kind, off], device_id=(src, slab), device_id_type=MESH)

    def forward(kind, off, t):
        src = partner(me, off, owners)
        source, target = pairs[kind]
        return pltpu.make_async_remote_copy(
            src_ref=target.at[slab, src] if off else source.at[me], dst_ref=target.at[slab, src],
            send_sem=fwd_send.at[kind, t, off], recv_sem=fwd_recv.at[kind, t, off],
            device_id=(me, lax.rem(slab + t, slabs)), device_id_type=MESH)

    def forwarded(kind, off, t):
        src = partner(me, off, owners)
        peer = lax.rem(slab - t + slabs, slabs)
        target = pairs[kind][1]
        return pltpu.make_async_remote_copy(
            src_ref=target.at[peer, src], dst_ref=target.at[peer, src], send_sem=fwd_send.at[kind, t, off],
            recv_sem=fwd_recv.at[kind, t, off], device_id=(me, peer), device_id_type=MESH)

    half = owners // 2
    order = [off for near in range(half) for off in ((half + near, near) if near else (half,))]
    own = [pltpu.make_async_copy(source.at[me], target.at[slab, me], own_sem.at[kind])
           for kind, (source, target) in enumerate(pairs)]
    for kind in range(2):
        for t in range(1, slabs):
            forward(kind, 0, t).start()
    for off in order:
        for kind in range(2):
            give(kind, off).start()
    for kind in range(2):
        own[kind].start()
    for off in order:
        for kind in range(2):
            given(kind, off).wait_recv()
            for t in range(1, slabs):
                forward(kind, off, t).start()
    for kind in range(2):
        own[kind].wait()
        for off in order:
            give(kind, off).wait_send()
        for off in [0] + order:
            for t in range(1, slabs):
                forward(kind, off, t).wait_send()
                forwarded(kind, off, t).wait_recv()


def finish_kernel(ids_ref, q_ref, meta_ref, cent_ref, out_ref, count_ref):
    contributions = q_ref.shape[0]
    share = cent_ref.shape[0]
    first = ids_ref[contributions] * share
    out_ref[...] = PRIOR_WEIGHT * unit_rows(cent_ref[...])
    count_ref[...] = jnp.zeros_like(count_ref)
    for start in range(0, contributions, 128):
        many = min(128, contributions - start)
        rows = jnp.concatenate([meta_ref[start : start + many, half, :] for half in range(CENT_BLK // 128)], axis=1)
        if many < 128:
            rows = jnp.concatenate([rows, jnp.zeros((128 - many, CENT_BLK), jnp.float32)], axis=0)
        scales = rows.T
        for k in range(many):
            inner = ids_ref[start + k] - first

            @pl.when((inner >= 0) & (inner < share))
            def _():
                out_ref[inner] += q_ref[start + k].astype(jnp.float32) * scales[:, k : k + 1]
                parts = [meta_ref[start + k, 2 + half : 3 + half, :] for half in range(CENT_BLK // 128)]
                count_ref[pl.ds(inner, 1), :] += jnp.concatenate(parts, axis=1)

    masses = jnp.concatenate([count_ref[...], jnp.zeros((128 - share, CENT_BLK), jnp.float32)], axis=0).T
    for i in range(share):
        out_ref[i] = out_ref[i] / (masses[:, i : i + 1] + PRIOR_WEIGHT)


def shards(owners, slabs, tokens, listed, centroids):
    width = tokens.shape[-1]
    blocks = listed.shape[0]
    per_owner = centroids.shape[0] // CENT_BLK
    share = per_owner // slabs
    cents = centroids.reshape(per_owner, CENT_BLK, width)
    vmem = pl.BlockSpec(memory_space=pltpu.VMEM)
    anywhere = pl.BlockSpec(memory_space=pl.ANY)
    dma = pltpu.SemaphoreType.DMA

    fetched, req = pl.pallas_call(
        functools.partial(fetch_kernel, owners),
        out_shape=(jax.ShapeDtypeStruct((owners, CENT_BLK, width), jnp.bfloat16),
                   jax.ShapeDtypeStruct((8, 128), jnp.int32)),
        in_specs=[vmem, vmem],
        out_specs=(anywhere, vmem),
        scratch_shapes=[
            pltpu.VMEM((owners, 8, 128), jnp.int32),
            pltpu.SMEM((owners, 128), jnp.int32),
            pltpu.VMEM((owners, CENT_BLK, width), jnp.bfloat16),
            dma((owners,)), dma((owners,)), dma, dma((owners,)), dma((owners,)), dma,
        ],
        compiler_params=pltpu.CompilerParams(
            collective_id=0, has_side_effects=True, vmem_limit_bytes=16 * 2**20),
        name="fetch",
    )(listed, cents)

    group = 4
    packed, meta = pl.pallas_call(
        functools.partial(softmax_kernel, group),
        out_shape=(jax.ShapeDtypeStruct((owners, CENT_BLK, width), jnp.int16),
                   jax.ShapeDtypeStruct((owners, 8, 128), jnp.float32)),
        grid_spec=pltpu.PrefetchScalarGridSpec(
            num_scalar_prefetch=2,
            grid=(blocks // group,),
            in_specs=[
                pl.BlockSpec((group, TOK_BLK, width), lambda i, *_: (i, 0, 0)),
                pl.BlockSpec((owners, CENT_BLK, width), lambda i, *_: (0, 0, 0)),
            ],
            out_specs=[
                pl.BlockSpec((owners, CENT_BLK, width), lambda i, *_: (0, 0, 0)),
                pl.BlockSpec((owners, 8, 128), lambda i, *_: (0, 0, 0)),
            ],
            scratch_shapes=[
                pltpu.VMEM((owners, CENT_BLK, width), jnp.float32),
                pltpu.VMEM((owners, CENT_BLK, 128), jnp.float32),
                pltpu.VMEM((2, 3, CENT_BLK, TOK_BLK), jnp.float32),
                pltpu.VMEM((2, TOK_BLK, width), jnp.bfloat16),
                pltpu.VMEM((2, 8, TOK_BLK), jnp.float32),
            ],
        ),
        compiler_params=pltpu.CompilerParams(
            dimension_semantics=("arbitrary",), vmem_limit_bytes=40 * 2**20),
        name="softmax",
    )((listed // per_owner).reshape(-1), req[0], tokens.reshape(blocks, TOK_BLK, width), fetched)

    q_all, meta_all = pl.pallas_call(
        functools.partial(return_kernel, owners, slabs),
        out_shape=(jax.ShapeDtypeStruct((slabs, owners, CENT_BLK, width), jnp.int16),
                   jax.ShapeDtypeStruct((slabs, owners, 8, 128), jnp.float32)),
        in_specs=[anywhere, anywhere],
        out_specs=(anywhere, anywhere),
        scratch_shapes=[dma((2, owners)), dma((2, owners)), dma((2, slabs, owners)), dma((2, slabs, owners)), dma((2,))],
        compiler_params=pltpu.CompilerParams(collective_id=1, has_side_effects=True),
        name="give_back",
    )(packed, meta)

    contributions = slabs * owners
    meta_flat = meta_all.reshape(contributions, 8, 128)
    ids = jnp.concatenate([meta_flat[:, 4, 0].astype(jnp.int32), lax.axis_index("slab").astype(jnp.int32)[None]])
    refined, counts = pl.pallas_call(
        finish_kernel,
        out_shape=(jax.ShapeDtypeStruct((share, CENT_BLK, width), jnp.float32),
                   jax.ShapeDtypeStruct((share, CENT_BLK), jnp.float32)),
        grid_spec=pltpu.PrefetchScalarGridSpec(
            num_scalar_prefetch=1,
            grid=(1,),
            in_specs=[
                pl.BlockSpec((contributions, CENT_BLK, width), lambda i, *_: (0, 0, 0)),
                pl.BlockSpec((contributions, 8, 128), lambda i, *_: (0, 0, 0)),
                pl.BlockSpec((share, CENT_BLK, width), lambda i, ids: (ids[contributions], 0, 0)),
            ],
            out_specs=[
                pl.BlockSpec((share, CENT_BLK, width), lambda i, *_: (0, 0, 0)),
                pl.BlockSpec((share, CENT_BLK), lambda i, *_: (0, 0)),
            ],
        ),
        compiler_params=pltpu.CompilerParams(
            dimension_semantics=("arbitrary",), vmem_limit_bytes=56 * 2**20),
        name="finish",
    )(ids, q_all.reshape(contributions, CENT_BLK, width), meta_flat, cents)
    return refined.reshape(share * CENT_BLK, width), counts.reshape(share * CENT_BLK)


def solution(mesh):
    placed = (P(("blk", "slab"), None), P(("blk", "slab"), None), P("blk", None))
    return jax.shard_map(
        functools.partial(shards, mesh.shape["blk"], mesh.shape["slab"]),
        mesh=mesh,
        in_specs=placed,
        out_specs=(P(("blk", "slab"), None), P(("blk", "slab"))),
        check_vma=False,
    )
```

```python
import functools
import math

import jax
import jax.numpy as jnp
from jax import lax
from jax.experimental import pallas as pl
from jax.experimental.pallas import tpu as pltpu
from jax.sharding import PartitionSpec as P

CENT_BLK = 256
TOK_BLK = 256
SOFTMAX_TEMP = 0.1
PRIOR_WEIGHT = 4.0
EPSILON = 1e-06
LEVELS = 32767.0
MESH = pl.DeviceIdType.MESH


def unit_rows(values):
    widened = values.astype(jnp.float32)
    return widened * lax.rsqrt(jnp.mean(widened * widened, axis=-1, keepdims=True) + EPSILON)


def partner(me, off, count):
    assert count & (count - 1) == 0
    other = 0
    bit = 1
    while bit < count:
        mine = lax.rem(me // bit, 2)
        other = other + bit * (1 - mine if off & bit else mine)
        bit *= 2
    return other


def greet(peers):
    barrier = pltpu.get_barrier_semaphore()
    for peer in peers:
        pl.semaphore_signal(barrier, inc=1, device_id=peer, device_id_type=MESH)
    pl.semaphore_wait(barrier, len(peers))


def fetch_kernel(owners, listed_ref, cent_ref, out_ref, req_ref, cents, asked_v, asked_s, reply, cent_sem,
                 ask_send, ask_recv, ask_local, rep_send, rep_recv, own_sem):
    me = lax.axis_index("blk")
    slab = lax.axis_index("slab")
    per_owner = cent_ref.shape[0]

    load = pltpu.make_async_copy(cent_ref, cents, cent_sem)
    load.start()
    rows = lax.broadcasted_iota(jnp.int32, (128, listed_ref.shape[1]), 0)
    best = jnp.zeros((128, 1), jnp.int32)
    for j in range(listed_ref.shape[0]):
        inner = listed_ref[j : j + 1, :] - rows * per_owner
        held = jnp.where((inner >= 0) & (inner < per_owner), inner + 1, 0)
        best = jnp.maximum(best, jnp.max(held, axis=1, keepdims=True))
    req_ref[...] = jnp.broadcast_to(best, (128, 128)).T[0:1]

    greet([(partner(me, off, owners), slab) for off in range(1, owners)])

    def ask(off):
        return pltpu.make_async_remote_copy(
            src_ref=req_ref, dst_ref=asked_v.at[me], send_sem=ask_send.at[off], recv_sem=ask_recv.at[off],
            device_id=(partner(me, off, owners), slab), device_id_type=MESH)

    def asked_by(off):
        src = partner(me, off, owners)
        return pltpu.make_async_remote_copy(
            src_ref=req_ref, dst_ref=asked_v.at[src], send_sem=ask_send.at[off], recv_sem=ask_recv.at[off],
            device_id=(src, slab), device_id_type=MESH)

    def give(off):
        return pltpu.make_async_remote_copy(
            src_ref=reply.at[off], dst_ref=out_ref.at[me], send_sem=rep_send.at[off], recv_sem=rep_recv.at[off],
            device_id=(partner(me, off, owners), slab), device_id_type=MESH)

    def given_by(off):
        src = partner(me, off, owners)
        return pltpu.make_async_remote_copy(
            src_ref=reply.at[off], dst_ref=out_ref.at[src], send_sem=rep_send.at[off], recv_sem=rep_recv.at[off],
            device_id=(src, slab), device_id_type=MESH)

    far_first = list(range(owners - 1, 0, -1))
    for off in far_first:
        ask(off).start()
    asked_v[me] = req_ref[...]
    for off in far_first:
        asked_by(off).wait_recv()
    pull = pltpu.make_async_copy(asked_v.at[:, 0], asked_s, ask_local)
    pull.start()
    pull.wait()
    own = pltpu.make_async_copy(reply.at[0], out_ref.at[me], own_sem)
    load.wait()
    for off in far_first + [0]:
        wanted = jnp.maximum(asked_s[partner(me, off, owners), me] - 1, 0)
        reply[off] = unit_rows(cents[wanted]).astype(jnp.bfloat16)
        (give(off) if off else own).start()
    own.wait()
    for off in far_first:
        ask(off).wait_send()
        give(off).wait_send()
        given_by(off).wait_recv()


def softmax_kernel(group, per_owner, listed_ref, req_ref, tok_ref, cent_ref, q_ref, meta_ref, total, mass, grown, tok_held, scales):
    step = pl.program_id(0)
    owners = cent_ref.shape[0]
    width = tok_ref.shape[-1]
    factor = math.log2(math.e) / (width * SOFTMAX_TEMP)

    @pl.when(step == 0)
    def _():
        total[...] = jnp.zeros_like(total)
        mass[...] = jnp.zeros_like(mass)
        grown[1] = jnp.zeros_like(grown[1])
        tok_held[1] = jnp.zeros_like(tok_held[1])
        scales[1] = jnp.zeros_like(scales[1])

    def collect(block, side):
        tok = tok_held[side]
        scale = scales[side, 0:1]
        for j in range(3):
            slot = lax.div(listed_ref[j, block], per_owner)
            weights = grown[side, j] * scale
            part = weights[:, :128]
            for lane in range(128, TOK_BLK, 128):
                part = part + weights[:, lane : lane + 128]
            mass[slot] += part
            total[slot] += jnp.dot(weights.astype(jnp.bfloat16), tok, preferred_element_type=jnp.float32)

    def grow(block, g, side):
        tok = unit_rows(tok_ref[g]).astype(jnp.bfloat16)
        tok_held[side] = tok
        norm = jnp.zeros((1, TOK_BLK), jnp.float32)
        for j in range(3):
            scores = lax.dot_general(cent_ref[lax.div(listed_ref[j, block], per_owner)], tok, (((1,), (1,)), ((), ())),
                                     preferred_element_type=jnp.float32)
            value = jnp.exp2(scores * factor)
            grown[side, j] = value
            norm = norm + jnp.sum(value, axis=0, keepdims=True)
        scales[side] = jnp.broadcast_to(1.0 / norm, (8, TOK_BLK))

    for g in range(group):
        block = step * group + g
        collect(jnp.maximum(block - 1, 0), (g + 1) % 2)
        grow(block, g, g % 2)

    @pl.when(step == pl.num_programs(0) - 1)
    def _():
        collect(step * group + group - 1, (group + 1) % 2)
        lanes = lax.broadcasted_iota(jnp.int32, (CENT_BLK, 128), 1)
        table = jnp.zeros((CENT_BLK, 128), jnp.float32)
        for k in range(owners):
            sums = total[k]
            top = jnp.max(jnp.abs(sums), axis=1, keepdims=True)
            inverse = LEVELS / jnp.maximum(top, 1e-30)
            q_ref[k] = jnp.floor(sums * inverse + 0.5).astype(jnp.int32).astype(jnp.int16)
            count = jnp.sum(mass[k], axis=1, keepdims=True)
            wanted = jnp.maximum(req_ref[0, k] - 1, 0).astype(jnp.float32)
            table = jnp.where(lanes == k, top * (1.0 / LEVELS), table)
            table = jnp.where(lanes == owners + k, count, table)
            table = jnp.where(lanes == 2 * owners + k, wanted, table)
        turned = table.T
        for kind in range(3):
            rows = turned[kind * owners : (kind + 1) * owners]
            for half in range(CENT_BLK // 128):
                meta_ref[:, 2 * kind + half, :] = rows[:, half * 128 : (half + 1) * 128]
        meta_ref[:, 6:, :] = jnp.zeros((owners, 2, 128), jnp.float32)


def return_kernel(owners, slabs, q_ref, meta_ref, q_out, meta_out, send_sem, recv_sem, fwd_send, fwd_recv, own_sem):
    me = lax.axis_index("blk")
    slab = lax.axis_index("slab")
    greet([(partner(me, off, owners), slab) for off in range(1, owners)]
          + [(me, lax.rem(slab + t, slabs)) for t in range(1, slabs)])
    pairs = ((q_ref, q_out), (meta_ref, meta_out))

    def give(kind, off):
        dest = partner(me, off, owners)
        source, target = pairs[kind]
        return pltpu.make_async_remote_copy(
            src_ref=source.at[dest], dst_ref=target.at[slab, me], send_sem=send_sem.at[kind, off],
            recv_sem=recv_sem.at[kind, off], device_id=(dest, slab), device_id_type=MESH)

    def given(kind, off):
        src = partner(me, off, owners)
        source, target = pairs[kind]
        return pltpu.make_async_remote_copy(
            src_ref=source.at[src], dst_ref=target.at[slab, src], send_sem=send_sem.at[kind, off],
            recv_sem=recv_sem.at[kind, off], device_id=(src, slab), device_id_type=MESH)

    def forward(kind, off, t):
        src = partner(me, off, owners)
        source, target = pairs[kind]
        return pltpu.make_async_remote_copy(
            src_ref=target.at[slab, src] if off else source.at[me], dst_ref=target.at[slab, src],
            send_sem=fwd_send.at[kind, t, off], recv_sem=fwd_recv.at[kind, t, off],
            device_id=(me, lax.rem(slab + t, slabs)), device_id_type=MESH)

    def forwarded(kind, off, t):
        src = partner(me, off, owners)
        peer = lax.rem(slab - t + slabs, slabs)
        target = pairs[kind][1]
        return pltpu.make_async_remote_copy(
            src_ref=target.at[peer, src], dst_ref=target.at[peer, src], send_sem=fwd_send.at[kind, t, off],
            recv_sem=fwd_recv.at[kind, t, off], device_id=(me, peer), device_id_type=MESH)

    half = owners // 2
    near, far = list(range(1, half)), list(range(half, owners))
    own = [pltpu.make_async_copy(source.at[me], target.at[slab, me], own_sem.at[kind])
           for kind, (source, target) in enumerate(pairs)]

    def send(off):
        for kind in (1, 0):
            give(kind, off).start()

    def pass_on(off):
        for kind in range(2):
            if off:
                given(kind, off).wait_recv()
            for t in range(1, slabs):
                forward(kind, off, t).start()

    pass_on(0)
    send(far[0])
    for off in near:
        send(off)
    send(far[1])
    for kind in range(2):
        own[kind].start()
    ready = list(near)
    for i, off in enumerate(far):
        pass_on_now, ready = ready[:2], ready[2:]
        for other in pass_on_now:
            pass_on(other)
        for kind in range(2):
            give(kind, off).wait_send()
        if i + 2 < len(far):
            send(far[i + 2])
        ready.append(off)
    for off in ready:
        pass_on(off)
    for kind in range(2):
        own[kind].wait()
        for off in near:
            give(kind, off).wait_send()
        for off in [0] + near + far:
            for t in range(1, slabs):
                forward(kind, off, t).wait_send()
                forwarded(kind, off, t).wait_recv()


def finish_kernel(q_ref, meta_ref, cent_ref, out_ref, count_ref, ids, cents, mass, id_sem, cent_sem):
    contributions = q_ref.shape[0]
    share = cents.shape[0]
    first = lax.axis_index("slab") * share
    pull = pltpu.make_async_copy(meta_ref.at[:, 4], ids, id_sem)
    pull.start()
    load = pltpu.make_async_copy(cent_ref.at[pl.ds(first, share)], cents, cent_sem)
    load.start()
    mass[...] = jnp.zeros_like(mass)
    load.wait()
    out_ref[...] = PRIOR_WEIGHT * unit_rows(cents[...])
    pull.wait()
    for start in range(0, contributions, 128):
        many = min(128, contributions - start)
        rows = jnp.concatenate([meta_ref[start : start + many, half, :] for half in range(CENT_BLK // 128)], axis=1)
        if many < 128:
            rows = jnp.concatenate([rows, jnp.zeros((128 - many, CENT_BLK), jnp.float32)], axis=0)
        scales = rows.T
        for k in range(many):
            inner = ids[start + k, 0].astype(jnp.int32) - first

            @pl.when((inner >= 0) & (inner < share))
            def _():
                out_ref[inner] += q_ref[start + k].astype(jnp.float32) * scales[:, k : k + 1]
                parts = [meta_ref[start + k, 2 + half : 3 + half, :] for half in range(CENT_BLK // 128)]
                mass[pl.ds(inner, 1), :] += jnp.concatenate(parts, axis=1)

    for half in range(CENT_BLK // 128):
        count_ref[:, half, :] = mass[:, half * 128 : (half + 1) * 128]
    masses = jnp.concatenate([mass[...], jnp.zeros((128 - share, CENT_BLK), jnp.float32)], axis=0).T
    for i in range(share):
        out_ref[i] = out_ref[i] / (masses[:, i : i + 1] + PRIOR_WEIGHT)


def shards(owners, slabs, tokens, listed, centroids):
    width = tokens.shape[-1]
    blocks = listed.shape[0]
    per_owner = centroids.shape[0] // CENT_BLK
    share = per_owner // slabs
    cents = centroids.reshape(per_owner, CENT_BLK, width)
    vmem = pl.BlockSpec(memory_space=pltpu.VMEM)
    anywhere = pl.BlockSpec(memory_space=pl.ANY)
    dma = pltpu.SemaphoreType.DMA

    fetched, req = pl.pallas_call(
        functools.partial(fetch_kernel, owners),
        out_shape=(jax.ShapeDtypeStruct((owners, CENT_BLK, width), jnp.bfloat16),
                   jax.ShapeDtypeStruct((1, 128), jnp.int32)),
        in_specs=[vmem, anywhere],
        out_specs=(anywhere, vmem),
        scratch_shapes=[
            pltpu.VMEM(cents.shape, cents.dtype),
            pltpu.VMEM((owners, 1, 128), jnp.int32),
            pltpu.SMEM((owners, 128), jnp.int32),
            pltpu.VMEM((owners, CENT_BLK, width), jnp.bfloat16),
            dma, dma((owners,)), dma((owners,)), dma, dma((owners,)), dma((owners,)), dma,
        ],
        compiler_params=pltpu.CompilerParams(
            collective_id=0, has_side_effects=True, vmem_limit_bytes=60 * 2**20),
        name="fetch",
    )(listed.T, cents)

    group = 4
    packed, meta = pl.pallas_call(
        functools.partial(softmax_kernel, group, per_owner),
        out_shape=(jax.ShapeDtypeStruct((owners, CENT_BLK, width), jnp.int16),
                   jax.ShapeDtypeStruct((owners, 8, 128), jnp.float32)),
        grid_spec=pltpu.PrefetchScalarGridSpec(
            num_scalar_prefetch=2,
            grid=(blocks // group,),
            in_specs=[
                pl.BlockSpec((group, TOK_BLK, width), lambda i, *_: (i, 0, 0)),
                pl.BlockSpec((owners, CENT_BLK, width), lambda i, *_: (0, 0, 0)),
            ],
            out_specs=[
                pl.BlockSpec((owners, CENT_BLK, width), lambda i, *_: (0, 0, 0)),
                pl.BlockSpec((owners, 8, 128), lambda i, *_: (0, 0, 0)),
            ],
            scratch_shapes=[
                pltpu.VMEM((owners, CENT_BLK, width), jnp.float32),
                pltpu.VMEM((owners, CENT_BLK, 128), jnp.float32),
                pltpu.VMEM((2, 3, CENT_BLK, TOK_BLK), jnp.float32),
                pltpu.VMEM((2, TOK_BLK, width), jnp.bfloat16),
                pltpu.VMEM((2, 8, TOK_BLK), jnp.float32),
            ],
        ),
        compiler_params=pltpu.CompilerParams(
            dimension_semantics=("arbitrary",), vmem_limit_bytes=60 * 2**20),
        name="softmax",
    )(listed.T, req, tokens.reshape(blocks, TOK_BLK, width), fetched)

    q_all, meta_all = pl.pallas_call(
        functools.partial(return_kernel, owners, slabs),
        out_shape=(jax.ShapeDtypeStruct((slabs, owners, CENT_BLK, width), jnp.int16),
                   jax.ShapeDtypeStruct((slabs, owners, 8, 128), jnp.float32)),
        in_specs=[anywhere, anywhere],
        out_specs=(anywhere, anywhere),
        scratch_shapes=[dma((2, owners)), dma((2, owners)), dma((2, slabs, owners)), dma((2, slabs, owners)), dma((2,))],
        compiler_params=pltpu.CompilerParams(
            collective_id=1, has_side_effects=True, vmem_limit_bytes=60 * 2**20),
        name="give_back",
    )(packed, meta)

    contributions = slabs * owners
    meta_flat = meta_all.reshape(contributions, 8, 128)
    refined, counts = pl.pallas_call(
        finish_kernel,
        out_shape=(jax.ShapeDtypeStruct((share, CENT_BLK, width), jnp.float32),
                   jax.ShapeDtypeStruct((share, CENT_BLK // 128, 128), jnp.float32)),
        in_specs=[vmem, vmem, anywhere],
        out_specs=(vmem, vmem),
        scratch_shapes=[
            pltpu.SMEM((contributions, 128), jnp.float32),
            pltpu.VMEM((share, CENT_BLK, width), cents.dtype),
            pltpu.VMEM((share, CENT_BLK), jnp.float32),
            dma, dma,
        ],
        compiler_params=pltpu.CompilerParams(vmem_limit_bytes=60 * 2**20),
        name="finish",
    )(q_all.reshape(contributions, CENT_BLK, width), meta_flat, cents)
    return refined.reshape(share * CENT_BLK, width), counts.reshape(share * CENT_BLK)


def solution(mesh):
    placed = (P(("blk", "slab"), None), P(("blk", "slab"), None), P("blk", None))
    return jax.shard_map(
        functools.partial(shards, mesh.shape["blk"], mesh.shape["slab"]),
        mesh=mesh,
        in_specs=placed,
        out_specs=(P(("blk", "slab"), None), P(("blk", "slab"))),
        check_vma=False,
    )
```

```python
import functools

import jax
import jax.numpy as jnp
from jax import lax
from jax.experimental import pallas as pl
from jax.experimental.pallas import tpu as pltpu
from jax.sharding import PartitionSpec as P

CENT_BLK = 256
TOK_BLK = 256
SOFTMAX_TEMP = 0.1
PRIOR_WEIGHT = 4.0
EPSILON = 1e-06
LEVELS = 32767.0
MESH = pl.DeviceIdType.MESH


def unit_rows(values):
    widened = values.astype(jnp.float32)
    return widened * lax.rsqrt(jnp.mean(widened * widened, axis=-1, keepdims=True) + EPSILON)


def partner(me, off, count):
    assert count & (count - 1) == 0
    other = 0
    bit = 1
    while bit < count:
        mine = lax.rem(me // bit, 2)
        other = other + bit * (1 - mine if off & bit else mine)
        bit *= 2
    return other


def greet(peers):
    barrier = pltpu.get_barrier_semaphore()
    for peer in peers:
        pl.semaphore_signal(barrier, inc=1, device_id=peer, device_id_type=MESH)
    pl.semaphore_wait(barrier, len(peers))


def fetch_kernel(owners, listed_ref, cent_ref, out_ref, req_ref, cents, asked_v, asked_s, reply, cent_sem,
                 ask_send, ask_recv, ask_local, rep_send, rep_recv, own_sem):
    me = lax.axis_index("blk")
    slab = lax.axis_index("slab")
    per_owner = cent_ref.shape[0]

    load = pltpu.make_async_copy(cent_ref, cents, cent_sem)
    load.start()
    rows = lax.broadcasted_iota(jnp.int32, (128, listed_ref.shape[1]), 0)
    best = jnp.zeros((128, 1), jnp.int32)
    for j in range(listed_ref.shape[0]):
        inner = listed_ref[j : j + 1, :] - rows * per_owner
        held = jnp.where((inner >= 0) & (inner < per_owner), inner + 1, 0)
        best = jnp.maximum(best, jnp.max(held, axis=1, keepdims=True))
    req_ref[...] = jnp.broadcast_to(best, (128, 128)).T[0:1]

    greet([(partner(me, off, owners), slab) for off in range(1, owners)])

    def ask(off):
        return pltpu.make_async_remote_copy(
            src_ref=req_ref, dst_ref=asked_v.at[me], send_sem=ask_send.at[off], recv_sem=ask_recv.at[off],
            device_id=(partner(me, off, owners), slab), device_id_type=MESH)

    def asked_by(off):
        src = partner(me, off, owners)
        return pltpu.make_async_remote_copy(
            src_ref=req_ref, dst_ref=asked_v.at[src], send_sem=ask_send.at[off], recv_sem=ask_recv.at[off],
            device_id=(src, slab), device_id_type=MESH)

    def give(off):
        return pltpu.make_async_remote_copy(
            src_ref=reply.at[off], dst_ref=out_ref.at[me], send_sem=rep_send.at[off], recv_sem=rep_recv.at[off],
            device_id=(partner(me, off, owners), slab), device_id_type=MESH)

    def given_by(off):
        src = partner(me, off, owners)
        return pltpu.make_async_remote_copy(
            src_ref=reply.at[off], dst_ref=out_ref.at[src], send_sem=rep_send.at[off], recv_sem=rep_recv.at[off],
            device_id=(src, slab), device_id_type=MESH)

    far_first = list(range(owners - 1, 0, -1))
    for off in far_first:
        ask(off).start()
    asked_v[me] = req_ref[...]
    for off in far_first:
        asked_by(off).wait_recv()
    pull = pltpu.make_async_copy(asked_v.at[:, 0], asked_s, ask_local)
    pull.start()
    pull.wait()
    own = pltpu.make_async_copy(reply.at[0], out_ref.at[me], own_sem)
    load.wait()
    for off in far_first + [0]:
        wanted = jnp.maximum(asked_s[partner(me, off, owners), me] - 1, 0)
        reply[off] = unit_rows(cents[wanted]).astype(jnp.bfloat16)
        (give(off) if off else own).start()
    own.wait()
    for off in far_first:
        ask(off).wait_send()
        give(off).wait_send()
        given_by(off).wait_recv()


def softmax_kernel(group, unroll, per_owner, listed_ref, req_ref, tok_ref, cent_ref, q_ref, meta_ref, total, mass, grown, tok_held, scales):
    step = pl.program_id(0)
    owners = cent_ref.shape[0]
    width = tok_ref.shape[-1]
    factor = 1.0 / (width * SOFTMAX_TEMP)
    assert per_owner & (per_owner - 1) == 0
    shift = per_owner.bit_length() - 1

    @pl.when(step == 0)
    def _():
        total[...] = jnp.zeros_like(total)
        mass[...] = jnp.zeros_like(mass)
        grown[1] = jnp.zeros_like(grown[1])
        tok_held[1] = jnp.zeros_like(tok_held[1])
        scales[1] = jnp.zeros_like(scales[1])

    def slot_of(j, block):
        return listed_ref[j, block] >> shift

    def collect(block, side):
        weights = grown[side] * scales[side, 0:1]
        part = weights[:, :128]
        for lane in range(128, TOK_BLK, 128):
            part = part + weights[:, lane : lane + 128]
        sums = jnp.dot(weights.astype(jnp.bfloat16), tok_held[side], preferred_element_type=jnp.float32)
        for j in range(3):
            slot = slot_of(j, block)
            mass[slot] += part[j * CENT_BLK : (j + 1) * CENT_BLK]
            total[slot] += sums[j * CENT_BLK : (j + 1) * CENT_BLK]

    def grow(block, g, side):
        tok = unit_rows(tok_ref[g]).astype(jnp.bfloat16)
        tok_held[side] = tok
        cents = jnp.concatenate([cent_ref[slot_of(j, block)] for j in range(3)], axis=0)
        scores = lax.dot_general(cents, tok, (((1,), (1,)), ((), ())), preferred_element_type=jnp.float32)
        value = jnp.exp(scores * factor)
        grown[side] = value
        scales[side] = jnp.broadcast_to(1.0 / jnp.sum(value, axis=0, keepdims=True), (8, TOK_BLK))

    @pl.loop(0, group // unroll)
    def _(turn):
        for u in range(unroll):
            g = turn * unroll + u
            block = step * group + g
            collect(jnp.maximum(block - 1, 0), (u + 1) % 2)
            grow(block, g, u % 2)

    @pl.when(step == pl.num_programs(0) - 1)
    def _():
        collect(step * group + group - 1, (group + 1) % 2)
        lanes = lax.broadcasted_iota(jnp.int32, (CENT_BLK, 128), 1)
        table = jnp.zeros((CENT_BLK, 128), jnp.float32)
        for k in range(owners):
            sums = total[k]
            top = jnp.max(jnp.abs(sums), axis=1, keepdims=True)
            inverse = LEVELS / jnp.maximum(top, 1e-30)
            q_ref[k] = jnp.floor(sums * inverse + 0.5).astype(jnp.int32).astype(jnp.int16)
            count = jnp.sum(mass[k], axis=1, keepdims=True)
            wanted = jnp.maximum(req_ref[0, k] - 1, 0).astype(jnp.float32)
            table = jnp.where(lanes == k, top * (1.0 / LEVELS), table)
            table = jnp.where(lanes == owners + k, count, table)
            table = jnp.where(lanes == 2 * owners + k, wanted, table)
        turned = table.T
        for kind in range(3):
            rows = turned[kind * owners : (kind + 1) * owners]
            for half in range(CENT_BLK // 128):
                meta_ref[:, 2 * kind + half, :] = rows[:, half * 128 : (half + 1) * 128]
        meta_ref[:, 6:, :] = jnp.zeros((owners, 2, 128), jnp.float32)


def return_kernel(owners, slabs, q_ref, meta_ref, q_out, meta_out, send_sem, recv_sem, fwd_send, fwd_recv, own_sem):
    me = lax.axis_index("blk")
    slab = lax.axis_index("slab")
    greet([(partner(me, off, owners), slab) for off in range(1, owners)]
          + [(me, lax.rem(slab + t, slabs)) for t in range(1, slabs)])
    pairs = ((q_ref, q_out), (meta_ref, meta_out))

    def give(kind, off):
        dest = partner(me, off, owners)
        source, target = pairs[kind]
        return pltpu.make_async_remote_copy(
            src_ref=source.at[dest], dst_ref=target.at[slab, me], send_sem=send_sem.at[kind, off],
            recv_sem=recv_sem.at[kind, off], device_id=(dest, slab), device_id_type=MESH)

    def given(kind, off):
        src = partner(me, off, owners)
        source, target = pairs[kind]
        return pltpu.make_async_remote_copy(
            src_ref=source.at[src], dst_ref=target.at[slab, src], send_sem=send_sem.at[kind, off],
            recv_sem=recv_sem.at[kind, off], device_id=(src, slab), device_id_type=MESH)

    def forward(kind, off, t):
        src = partner(me, off, owners)
        source, target = pairs[kind]
        return pltpu.make_async_remote_copy(
            src_ref=target.at[slab, src] if off else source.at[me], dst_ref=target.at[slab, src],
            send_sem=fwd_send.at[kind, t, off], recv_sem=fwd_recv.at[kind, t, off],
            device_id=(me, lax.rem(slab + t, slabs)), device_id_type=MESH)

    def forwarded(kind, off, t):
        src = partner(me, off, owners)
        peer = lax.rem(slab - t + slabs, slabs)
        target = pairs[kind][1]
        return pltpu.make_async_remote_copy(
            src_ref=target.at[peer, src], dst_ref=target.at[peer, src], send_sem=fwd_send.at[kind, t, off],
            recv_sem=fwd_recv.at[kind, t, off], device_id=(me, peer), device_id_type=MESH)

    half = owners // 2
    near, far = list(range(1, half)), list(range(half, owners))
    own = [pltpu.make_async_copy(source.at[me], target.at[slab, me], own_sem.at[kind])
           for kind, (source, target) in enumerate(pairs)]

    def send(off):
        for kind in (1, 0):
            give(kind, off).start()

    def pass_on(off):
        for kind in range(2):
            if off:
                given(kind, off).wait_recv()
            for t in range(1, slabs):
                forward(kind, off, t).start()

    window = 3
    pass_on(0)
    for i in range(max(len(near), window)):
        if i < len(near):
            send(near[i])
        if i < min(window, len(far)):
            send(far[i])
        if i == 1:
            pass_on(near[0])
    for kind in range(2):
        own[kind].start()
    ready = near[1:]
    for i, off in enumerate(far):
        pass_on_now, ready = ready[:2], ready[2:]
        for other in pass_on_now:
            pass_on(other)
        for kind in range(2):
            give(kind, off).wait_send()
        if i + window < len(far):
            send(far[i + window])
        ready.append(off)
    for off in ready:
        pass_on(off)
    for kind in range(2):
        own[kind].wait()
        for off in near:
            give(kind, off).wait_send()
        for off in [0] + near + far:
            for t in range(1, slabs):
                forward(kind, off, t).wait_send()
                forwarded(kind, off, t).wait_recv()


def finish_kernel(q_ref, meta_ref, cent_ref, out_ref, count_ref, ids, cents, mass, id_sem, cent_sem):
    contributions = q_ref.shape[0]
    share = cents.shape[0]
    first = lax.axis_index("slab") * share
    pull = pltpu.make_async_copy(meta_ref.at[:, 4], ids, id_sem)
    pull.start()
    load = pltpu.make_async_copy(cent_ref.at[pl.ds(first, share)], cents, cent_sem)
    load.start()
    mass[...] = jnp.zeros_like(mass)
    load.wait()
    for i in range(share):
        out_ref[i] = PRIOR_WEIGHT * unit_rows(cents[i])
    pull.wait()
    for start in range(0, contributions, 128):
        many = min(128, contributions - start)
        rows = jnp.concatenate([meta_ref[start : start + many, half, :] for half in range(CENT_BLK // 128)], axis=1)
        if many < 128:
            rows = jnp.concatenate([rows, jnp.zeros((128 - many, CENT_BLK), jnp.float32)], axis=0)
        scales = rows.T
        for k in range(many):
            inner = ids[start + k, 0].astype(jnp.int32) - first

            @pl.when((inner >= 0) & (inner < share))
            def _():
                out_ref[inner] += q_ref[start + k].astype(jnp.float32) * scales[:, k : k + 1]
                parts = [meta_ref[start + k, 2 + half : 3 + half, :] for half in range(CENT_BLK // 128)]
                mass[pl.ds(inner, 1), :] += jnp.concatenate(parts, axis=1)

    for half in range(CENT_BLK // 128):
        count_ref[:, half, :] = mass[:, half * 128 : (half + 1) * 128]
    masses = jnp.concatenate([mass[...], jnp.zeros((128 - share, CENT_BLK), jnp.float32)], axis=0).T
    inverse = 1.0 / (masses + PRIOR_WEIGHT)
    for i in range(share):
        out_ref[i] = out_ref[i] * inverse[:, i : i + 1]


def shards(owners, slabs, tokens, listed, centroids):
    width = tokens.shape[-1]
    blocks = listed.shape[0]
    per_owner = centroids.shape[0] // CENT_BLK
    share = per_owner // slabs
    cents = centroids.reshape(per_owner, CENT_BLK, width)
    vmem = pl.BlockSpec(memory_space=pltpu.VMEM)
    anywhere = pl.BlockSpec(memory_space=pl.ANY)
    dma = pltpu.SemaphoreType.DMA

    fetched, req = pl.pallas_call(
        functools.partial(fetch_kernel, owners),
        out_shape=(jax.ShapeDtypeStruct((owners, CENT_BLK, width), jnp.bfloat16),
                   jax.ShapeDtypeStruct((1, 128), jnp.int32)),
        in_specs=[vmem, anywhere],
        out_specs=(anywhere, vmem),
        scratch_shapes=[
            pltpu.VMEM(cents.shape, cents.dtype),
            pltpu.VMEM((owners, 1, 128), jnp.int32),
            pltpu.SMEM((owners, 128), jnp.int32),
            pltpu.VMEM((owners, CENT_BLK, width), jnp.bfloat16),
            dma, dma((owners,)), dma((owners,)), dma, dma((owners,)), dma((owners,)), dma,
        ],
        compiler_params=pltpu.CompilerParams(
            collective_id=0, has_side_effects=True, vmem_limit_bytes=60 * 2**20),
        name="fetch",
    )(listed.T, cents)

    group = min(16, blocks)
    unroll = 4
    packed, meta = pl.pallas_call(
        functools.partial(softmax_kernel, group, unroll, per_owner),
        out_shape=(jax.ShapeDtypeStruct((owners, CENT_BLK, width), jnp.int16),
                   jax.ShapeDtypeStruct((owners, 8, 128), jnp.float32)),
        grid_spec=pltpu.PrefetchScalarGridSpec(
            num_scalar_prefetch=2,
            grid=(blocks // group,),
            in_specs=[
                pl.BlockSpec((group, TOK_BLK, width), lambda i, *_: (i, 0, 0)),
                pl.BlockSpec((owners, CENT_BLK, width), lambda i, *_: (0, 0, 0)),
            ],
            out_specs=[
                pl.BlockSpec((owners, CENT_BLK, width), lambda i, *_: (0, 0, 0)),
                pl.BlockSpec((owners, 8, 128), lambda i, *_: (0, 0, 0)),
            ],
            scratch_shapes=[
                pltpu.VMEM((owners, CENT_BLK, width), jnp.float32),
                pltpu.VMEM((owners, CENT_BLK, 128), jnp.float32),
                pltpu.VMEM((2, 3 * CENT_BLK, TOK_BLK), jnp.float32),
                pltpu.VMEM((2, TOK_BLK, width), jnp.bfloat16),
                pltpu.VMEM((2, 8, TOK_BLK), jnp.float32),
            ],
        ),
        compiler_params=pltpu.CompilerParams(
            dimension_semantics=("arbitrary",), vmem_limit_bytes=60 * 2**20),
        name="softmax",
    )(listed.T, req, tokens.reshape(blocks, TOK_BLK, width), fetched)

    q_all, meta_all = pl.pallas_call(
        functools.partial(return_kernel, owners, slabs),
        out_shape=(jax.ShapeDtypeStruct((slabs, owners, CENT_BLK, width), jnp.int16),
                   jax.ShapeDtypeStruct((slabs, owners, 8, 128), jnp.float32)),
        in_specs=[anywhere, anywhere],
        out_specs=(anywhere, anywhere),
        scratch_shapes=[dma((2, owners)), dma((2, owners)), dma((2, slabs, owners)), dma((2, slabs, owners)), dma((2,))],
        compiler_params=pltpu.CompilerParams(
            collective_id=1, has_side_effects=True, vmem_limit_bytes=60 * 2**20),
        name="give_back",
    )(packed, meta)

    contributions = slabs * owners
    meta_flat = meta_all.reshape(contributions, 8, 128)
    refined, counts = pl.pallas_call(
        finish_kernel,
        out_shape=(jax.ShapeDtypeStruct((share, CENT_BLK, width), jnp.float32),
                   jax.ShapeDtypeStruct((share, CENT_BLK // 128, 128), jnp.float32)),
        in_specs=[vmem, vmem, anywhere],
        out_specs=(vmem, vmem),
        scratch_shapes=[
            pltpu.SMEM((contributions, 128), jnp.float32),
            pltpu.VMEM((share, CENT_BLK, width), cents.dtype),
            pltpu.VMEM((share, CENT_BLK), jnp.float32),
            dma, dma,
        ],
        compiler_params=pltpu.CompilerParams(vmem_limit_bytes=60 * 2**20),
        name="finish",
    )(q_all.reshape(contributions, CENT_BLK, width), meta_flat, cents)
    return refined.reshape(share * CENT_BLK, width), counts.reshape(share * CENT_BLK)


def solution(mesh):
    placed = (P(("blk", "slab"), None), P(("blk", "slab"), None), P("blk", None))
    return jax.shard_map(
        functools.partial(shards, mesh.shape["blk"], mesh.shape["slab"]),
        mesh=mesh,
        in_specs=placed,
        out_specs=(P(("blk", "slab"), None), P(("blk", "slab"))),
        check_vma=False,
    )
```

```python
import functools

import jax
import jax.numpy as jnp
from jax import lax
from jax.experimental import pallas as pl
from jax.experimental.pallas import tpu as pltpu
from jax.sharding import PartitionSpec as P

CENT_BLK = 256
TOK_BLK = 256
SOFTMAX_TEMP = 0.1
PRIOR_WEIGHT = 4.0
EPSILON = 1e-06
LEVELS = 32767.0
MESH = pl.DeviceIdType.MESH


def unit_rows(values):
    widened = values.astype(jnp.float32)
    return widened * lax.rsqrt(jnp.mean(widened * widened, axis=-1, keepdims=True) + EPSILON)


def partner(me, off, count):
    assert count & (count - 1) == 0
    other = 0
    bit = 1
    while bit < count:
        mine = lax.rem(me // bit, 2)
        other = other + bit * (1 - mine if off & bit else mine)
        bit *= 2
    return other


def greet(peers):
    barrier = pltpu.get_barrier_semaphore()
    for peer in peers:
        pl.semaphore_signal(barrier, inc=1, device_id=peer, device_id_type=MESH)
    pl.semaphore_wait(barrier, len(peers))


def fetch_kernel(owners, listed_ref, cent_ref, out_ref, req_ref, cents, asked_v, asked_s, reply, cent_sem,
                 ask_send, ask_recv, ask_local, rep_send, rep_recv, own_sem):
    me = lax.axis_index("blk")
    slab = lax.axis_index("slab")
    per_owner = cent_ref.shape[0]

    load = pltpu.make_async_copy(cent_ref, cents, cent_sem)
    load.start()
    rows = lax.broadcasted_iota(jnp.int32, (128, listed_ref.shape[1]), 0)
    best = jnp.zeros((128, 1), jnp.int32)
    for j in range(listed_ref.shape[0]):
        inner = listed_ref[j : j + 1, :] - rows * per_owner
        held = jnp.where((inner >= 0) & (inner < per_owner), inner + 1, 0)
        best = jnp.maximum(best, jnp.max(held, axis=1, keepdims=True))
    req_ref[...] = jnp.broadcast_to(best, (128, 128)).T[0:1]

    greet([(partner(me, off, owners), slab) for off in range(1, owners)])

    def ask(off):
        return pltpu.make_async_remote_copy(
            src_ref=req_ref, dst_ref=asked_v.at[me], send_sem=ask_send.at[off], recv_sem=ask_recv.at[off],
            device_id=(partner(me, off, owners), slab), device_id_type=MESH)

    def asked_by(off):
        src = partner(me, off, owners)
        return pltpu.make_async_remote_copy(
            src_ref=req_ref, dst_ref=asked_v.at[src], send_sem=ask_send.at[off], recv_sem=ask_recv.at[off],
            device_id=(src, slab), device_id_type=MESH)

    def give(off):
        return pltpu.make_async_remote_copy(
            src_ref=reply.at[off], dst_ref=out_ref.at[me], send_sem=rep_send.at[off], recv_sem=rep_recv.at[off],
            device_id=(partner(me, off, owners), slab), device_id_type=MESH)

    def given_by(off):
        src = partner(me, off, owners)
        return pltpu.make_async_remote_copy(
            src_ref=reply.at[off], dst_ref=out_ref.at[src], send_sem=rep_send.at[off], recv_sem=rep_recv.at[off],
            device_id=(src, slab), device_id_type=MESH)

    far_first = list(range(owners - 1, 0, -1))
    for off in far_first:
        ask(off).start()
    asked_v[me] = req_ref[...]
    for off in far_first:
        asked_by(off).wait_recv()
    pull = pltpu.make_async_copy(asked_v.at[:, 0], asked_s, ask_local)
    pull.start()
    pull.wait()
    own = pltpu.make_async_copy(reply.at[0], out_ref.at[me], own_sem)
    load.wait()
    for off in far_first + [0]:
        wanted = jnp.maximum(asked_s[partner(me, off, owners), me] - 1, 0)
        reply[off] = unit_rows(cents[wanted]).astype(jnp.bfloat16)
        (give(off) if off else own).start()
    own.wait()
    for off in far_first:
        ask(off).wait_send()
        give(off).wait_send()
        given_by(off).wait_recv()


def softmax_kernel(group, unroll, per_owner, listed_ref, req_ref, tok_ref, cent_ref, q_ref, meta_ref, total, mass, grown, tok_held, scales):
    step = pl.program_id(0)
    owners = cent_ref.shape[0]
    width = tok_ref.shape[-1]
    factor = 1.0 / (width * SOFTMAX_TEMP)
    assert per_owner & (per_owner - 1) == 0
    shift = per_owner.bit_length() - 1

    @pl.when(step == 0)
    def _():
        total[...] = jnp.zeros_like(total)
        mass[...] = jnp.zeros_like(mass)
        grown[1] = jnp.zeros_like(grown[1])
        tok_held[1] = jnp.zeros_like(tok_held[1])
        scales[1] = jnp.zeros_like(scales[1])

    def slot_of(j, block):
        return listed_ref[j, block] >> shift

    def collect(block, side):
        weights = grown[side] * scales[side, 0:1]
        part = weights[:, :128]
        for lane in range(128, TOK_BLK, 128):
            part = part + weights[:, lane : lane + 128]
        sums = jnp.dot(weights.astype(jnp.bfloat16), tok_held[side], preferred_element_type=jnp.float32)
        for j in range(3):
            slot = slot_of(j, block)
            mass[slot] += part[j * CENT_BLK : (j + 1) * CENT_BLK]
            total[slot] += sums[j * CENT_BLK : (j + 1) * CENT_BLK]

    def grow(block, g, side):
        tok = unit_rows(tok_ref[g]).astype(jnp.bfloat16)
        tok_held[side] = tok
        cents = jnp.concatenate([cent_ref[slot_of(j, block)] for j in range(3)], axis=0)
        scores = lax.dot_general(cents, tok, (((1,), (1,)), ((), ())), preferred_element_type=jnp.float32)
        value = jnp.exp(scores * factor)
        grown[side] = value
        scales[side] = jnp.broadcast_to(1.0 / jnp.sum(value, axis=0, keepdims=True), (8, TOK_BLK))

    @pl.loop(0, group // unroll)
    def _(turn):
        for u in range(unroll):
            g = turn * unroll + u
            block = step * group + g
            collect(jnp.maximum(block - 1, 0), (u + 1) % 2)
            grow(block, g, u % 2)

    @pl.when(step == pl.num_programs(0) - 1)
    def _():
        collect(step * group + group - 1, (group + 1) % 2)
        lanes = lax.broadcasted_iota(jnp.int32, (CENT_BLK, 128), 1)
        table = jnp.zeros((CENT_BLK, 128), jnp.float32)
        for k in range(owners):
            sums = total[k]
            top = jnp.max(jnp.abs(sums), axis=1, keepdims=True)
            inverse = LEVELS / jnp.maximum(top, 1e-30)
            q_ref[k] = jnp.floor(sums * inverse + 0.5).astype(jnp.int32).astype(jnp.int16)
            count = jnp.sum(mass[k], axis=1, keepdims=True)
            wanted = jnp.maximum(req_ref[0, k] - 1, 0).astype(jnp.float32)
            table = jnp.where(lanes == k, top * (1.0 / LEVELS), table)
            table = jnp.where(lanes == owners + k, count, table)
            table = jnp.where(lanes == 2 * owners + k, wanted, table)
        turned = table.T
        for kind in range(3):
            rows = turned[kind * owners : (kind + 1) * owners]
            for half in range(CENT_BLK // 128):
                meta_ref[:, 2 * kind + half, :] = rows[:, half * 128 : (half + 1) * 128]
        meta_ref[:, 6:, :] = jnp.zeros((owners, 2, 128), jnp.float32)


def return_kernel(owners, slabs, q_ref, meta_ref, q_out, meta_out, send_sem, recv_sem, fwd_send, fwd_recv, own_sem):
    me = lax.axis_index("blk")
    slab = lax.axis_index("slab")
    greet([(partner(me, off, owners), slab) for off in range(1, owners)]
          + [(me, lax.rem(slab + t, slabs)) for t in range(1, slabs)])
    pairs = ((q_ref, q_out), (meta_ref, meta_out))

    def give(kind, off):
        dest = partner(me, off, owners)
        source, target = pairs[kind]
        return pltpu.make_async_remote_copy(
            src_ref=source.at[dest], dst_ref=target.at[slab, me], send_sem=send_sem.at[kind, off],
            recv_sem=recv_sem.at[kind, off], device_id=(dest, slab), device_id_type=MESH)

    def given(kind, off):
        src = partner(me, off, owners)
        source, target = pairs[kind]
        return pltpu.make_async_remote_copy(
            src_ref=source.at[src], dst_ref=target.at[slab, src], send_sem=send_sem.at[kind, off],
            recv_sem=recv_sem.at[kind, off], device_id=(src, slab), device_id_type=MESH)

    def forward(kind, off, t):
        src = partner(me, off, owners)
        source, target = pairs[kind]
        return pltpu.make_async_remote_copy(
            src_ref=target.at[slab, src] if off else source.at[me], dst_ref=target.at[slab, src],
            send_sem=fwd_send.at[kind, t, off], recv_sem=fwd_recv.at[kind, t, off],
            device_id=(me, lax.rem(slab + t, slabs)), device_id_type=MESH)

    def forwarded(kind, off, t):
        src = partner(me, off, owners)
        peer = lax.rem(slab - t + slabs, slabs)
        target = pairs[kind][1]
        return pltpu.make_async_remote_copy(
            src_ref=target.at[peer, src], dst_ref=target.at[peer, src], send_sem=fwd_send.at[kind, t, off],
            recv_sem=fwd_recv.at[kind, t, off], device_id=(me, peer), device_id_type=MESH)

    half = owners // 2
    near, far = list(range(1, half)), list(range(half, owners))
    own = [pltpu.make_async_copy(source.at[me], target.at[slab, me], own_sem.at[kind])
           for kind, (source, target) in enumerate(pairs)]

    def send(off):
        for kind in (1, 0):
            give(kind, off).start()

    def pass_on(off):
        for kind in range(2):
            if off:
                given(kind, off).wait_recv()
            for t in range(1, slabs):
                forward(kind, off, t).start()

    window = 3
    pass_on(0)
    for i in range(max(len(near), window)):
        if i < len(near):
            send(near[i])
        if i < min(window, len(far)):
            send(far[i])
        if i == 1:
            pass_on(near[0])
    for kind in range(2):
        own[kind].start()
    ready = near[1:]
    for i, off in enumerate(far):
        pass_on_now, ready = ready[:2], ready[2:]
        for other in pass_on_now:
            pass_on(other)
        for kind in range(2):
            give(kind, off).wait_send()
        if i + window < len(far):
            send(far[i + window])
        ready.append(off)
    for off in ready:
        pass_on(off)
    for kind in range(2):
        own[kind].wait()
        for off in near:
            give(kind, off).wait_send()
        for off in [0] + near + far:
            for t in range(1, slabs):
                forward(kind, off, t).wait_send()
                forwarded(kind, off, t).wait_recv()


def finish_kernel(q_hbm, meta_ref, cent_ref, out_hbm, count_ref, ids, cents, mass, q_ref, out_ref,
                  id_sem, cent_sem, q_sem, out_sem):
    contributions = q_ref.shape[0]
    share = cents.shape[0]
    first = lax.axis_index("slab") * share
    pull = pltpu.make_async_copy(meta_ref.at[:, 4], ids, id_sem)
    pull.start()
    load = pltpu.make_async_copy(cent_ref.at[pl.ds(first, share)], cents, cent_sem)
    load.start()
    bring = pltpu.make_async_copy(q_hbm, q_ref, q_sem)
    bring.start()
    mass[...] = jnp.zeros_like(mass)
    load.wait()
    for i in range(share):
        out_ref[i] = PRIOR_WEIGHT * unit_rows(cents[i])
    pull.wait()
    bring.wait()
    for start in range(0, contributions, 128):
        many = min(128, contributions - start)
        rows = jnp.concatenate([meta_ref[start : start + many, half, :] for half in range(CENT_BLK // 128)], axis=1)
        if many < 128:
            rows = jnp.concatenate([rows, jnp.zeros((128 - many, CENT_BLK), jnp.float32)], axis=0)
        scales = rows.T
        for k in range(many):
            inner = ids[start + k, 0].astype(jnp.int32) - first

            @pl.when((inner >= 0) & (inner < share))
            def _():
                out_ref[inner] += q_ref[start + k].astype(jnp.float32) * scales[:, k : k + 1]
                parts = [meta_ref[start + k, 2 + half : 3 + half, :] for half in range(CENT_BLK // 128)]
                mass[pl.ds(inner, 1), :] += jnp.concatenate(parts, axis=1)

    for half in range(CENT_BLK // 128):
        count_ref[:, half, :] = mass[:, half * 128 : (half + 1) * 128]
    masses = jnp.concatenate([mass[...], jnp.zeros((128 - share, CENT_BLK), jnp.float32)], axis=0).T
    inverse = 1.0 / (masses + PRIOR_WEIGHT)
    leave = [pltpu.make_async_copy(out_ref.at[i], out_hbm.at[i], out_sem.at[i]) for i in range(share)]
    for i in range(share):
        out_ref[i] = out_ref[i] * inverse[:, i : i + 1]
        leave[i].start()
    for i in range(share):
        leave[i].wait()


def shards(owners, slabs, tokens, listed, centroids):
    width = tokens.shape[-1]
    blocks = listed.shape[0]
    per_owner = centroids.shape[0] // CENT_BLK
    share = per_owner // slabs
    cents = centroids.reshape(per_owner, CENT_BLK, width)
    vmem = pl.BlockSpec(memory_space=pltpu.VMEM)
    anywhere = pl.BlockSpec(memory_space=pl.ANY)
    dma = pltpu.SemaphoreType.DMA

    fetched, req = pl.pallas_call(
        functools.partial(fetch_kernel, owners),
        out_shape=(jax.ShapeDtypeStruct((owners, CENT_BLK, width), jnp.bfloat16),
                   jax.ShapeDtypeStruct((1, 128), jnp.int32)),
        in_specs=[vmem, anywhere],
        out_specs=(anywhere, vmem),
        scratch_shapes=[
            pltpu.VMEM(cents.shape, cents.dtype),
            pltpu.VMEM((owners, 1, 128), jnp.int32),
            pltpu.SMEM((owners, 128), jnp.int32),
            pltpu.VMEM((owners, CENT_BLK, width), jnp.bfloat16),
            dma, dma((owners,)), dma((owners,)), dma, dma((owners,)), dma((owners,)), dma,
        ],
        compiler_params=pltpu.CompilerParams(
            collective_id=0, has_side_effects=True, vmem_limit_bytes=60 * 2**20),
        name="fetch",
    )(listed.T, cents)

    group = min(16, blocks)
    unroll = 8
    packed, meta = pl.pallas_call(
        functools.partial(softmax_kernel, group, unroll, per_owner),
        out_shape=(jax.ShapeDtypeStruct((owners, CENT_BLK, width), jnp.int16),
                   jax.ShapeDtypeStruct((owners, 8, 128), jnp.float32)),
        grid_spec=pltpu.PrefetchScalarGridSpec(
            num_scalar_prefetch=2,
            grid=(blocks // group,),
            in_specs=[
                pl.BlockSpec((group, TOK_BLK, width), lambda i, *_: (i, 0, 0)),
                pl.BlockSpec((owners, CENT_BLK, width), lambda i, *_: (0, 0, 0)),
            ],
            out_specs=[
                pl.BlockSpec((owners, CENT_BLK, width), lambda i, *_: (0, 0, 0)),
                pl.BlockSpec((owners, 8, 128), lambda i, *_: (0, 0, 0)),
            ],
            scratch_shapes=[
                pltpu.VMEM((owners, CENT_BLK, width), jnp.float32),
                pltpu.VMEM((owners, CENT_BLK, 128), jnp.float32),
                pltpu.VMEM((2, 3 * CENT_BLK, TOK_BLK), jnp.float32),
                pltpu.VMEM((2, TOK_BLK, width), jnp.bfloat16),
                pltpu.VMEM((2, 8, TOK_BLK), jnp.float32),
            ],
        ),
        compiler_params=pltpu.CompilerParams(
            dimension_semantics=("arbitrary",), vmem_limit_bytes=60 * 2**20),
        name="softmax",
    )(listed.T, req, tokens.reshape(blocks, TOK_BLK, width), fetched)

    q_all, meta_all = pl.pallas_call(
        functools.partial(return_kernel, owners, slabs),
        out_shape=(jax.ShapeDtypeStruct((slabs, owners, CENT_BLK, width), jnp.int16),
                   jax.ShapeDtypeStruct((slabs, owners, 8, 128), jnp.float32)),
        in_specs=[anywhere, anywhere],
        out_specs=(anywhere, anywhere),
        scratch_shapes=[dma((2, owners)), dma((2, owners)), dma((2, slabs, owners)), dma((2, slabs, owners)), dma((2,))],
        compiler_params=pltpu.CompilerParams(
            collective_id=1, has_side_effects=True, vmem_limit_bytes=60 * 2**20),
        name="give_back",
    )(packed, meta)

    contributions = slabs * owners
    meta_flat = meta_all.reshape(contributions, 8, 128)
    refined, counts = pl.pallas_call(
        finish_kernel,
        out_shape=(jax.ShapeDtypeStruct((share, CENT_BLK, width), jnp.float32),
                   jax.ShapeDtypeStruct((share, CENT_BLK // 128, 128), jnp.float32)),
        in_specs=[anywhere, vmem, anywhere],
        out_specs=(anywhere, vmem),
        scratch_shapes=[
            pltpu.SMEM((contributions, 128), jnp.float32),
            pltpu.VMEM((share, CENT_BLK, width), cents.dtype),
            pltpu.VMEM((share, CENT_BLK), jnp.float32),
            pltpu.VMEM((contributions, CENT_BLK, width), jnp.int16),
            pltpu.VMEM((share, CENT_BLK, width), jnp.float32),
            dma, dma, dma, dma((share,)),
        ],
        compiler_params=pltpu.CompilerParams(vmem_limit_bytes=60 * 2**20),
        name="finish",
    )(q_all.reshape(contributions, CENT_BLK, width), meta_flat, cents)
    return refined.reshape(share * CENT_BLK, width), counts.reshape(share * CENT_BLK)


def solution(mesh):
    placed = (P(("blk", "slab"), None), P(("blk", "slab"), None), P("blk", None))
    return jax.shard_map(
        functools.partial(shards, mesh.shape["blk"], mesh.shape["slab"]),
        mesh=mesh,
        in_specs=placed,
        out_specs=(P(("blk", "slab"), None), P(("blk", "slab"))),
        check_vma=False,
    )
```
